32 devices in a mesh: groups: 2 (over x), ab: 16 (over z, y, core).
Axes of the slice: x: 2, y: 2, z: 4, core: 2. Of those that a mesh axis runs over, the one named last changes fastest.
Arguments:
- amplitudes: bfloat16 [512, 32768], P(('groups', 'ab')), parts along dimension 0, may hold values from -6 to 6
- integrals: bfloat16 [4096, 32768], P('groups', 'ab'), parts along dimension 0, may hold values from -0.0625 to 0.0625
- block_mask: int32 [32, 256], P('groups', 'ab'), parts along dimension 0, may hold values 0 or 1
- pair_list: int32 [512], P('groups'), parts along dimension 0, may hold values from 0 to 255, each once
Outputs:
- residual: float32 [4096, 256], P(('groups', 'ab')), parts along dimension 0
The draws below stay inside these ranges and needn't reach their ends.
There are 2 independent parts, one for each index of `groups`. The reference program is written for one: setup_inputs(seed, part) draws one part's arguments, and reference() takes and returns one part's arrays. A program takes and returns all parts, laid end to end along the dimension named above; each array names one. Nothing has to cross between parts.
Inputs may be any that keep to these rules, and one draw needn't show every extreme that they name: `pair_list`: a permutation of the pair positions.
All inputs are finite; a program needn't handle non-finite values. No bound on the sum of `block_mask` on one device may be relied on, other than what follows from the above.
Results may differ from the reference program's by a relative error of at most 0.0003.
Values may be sent and summed in bfloat16 or wider, within the bound.
No kernel may reach another device: no remote copies, remote signals or barrier semaphores. Data moves between devices by JAX's collectives and lax.ppermute only.
A program may use at most 128 MiB of HBM per device.

```python
import jax
import jax.numpy as jnp
from jax import lax

TILE = 128
PAIRS = 256
AB = 2048
CD = 32768
AB_TILES = 16
CD_TILES = 256


def plant(values, stream_key, smallest, high):
    longest = values.shape.index(max(values.shape))
    spots = []
    for shift in (0, 1):
        where = [jax.random.randint(jax.random.fold_in(stream_key, axis), (), 0, length) for axis, length in enumerate(values.shape)]
        where[longest] = (where[longest] + shift) % values.shape[longest]
        spots.append(tuple(where))
    return values.at[spots[0]].set(smallest).at[spots[1]].set(high)


def strengthened(values, rng, source, target, shards_of, factor):
    def block_of(dim):
        return (jnp.arange(values.shape[dim]) // (values.shape[dim] // shards_of)).reshape((-1,) + (1,) * (values.ndim - 1 - dim))

    near = jax.random.permutation(rng, shards_of)[block_of(target)]
    second = (block_of(target) + shards_of // 2) % shards_of
    return jnp.where((block_of(source) == near) | (block_of(source) == second), factor * values, values)


def levels(rng, extent, split, smallest, high):
    gain, own = 1.0, jax.random.fold_in(rng, 6)
    for dim, parts in split:
        heights = jnp.exp(jax.random.uniform(jax.random.fold_in(own, dim), (parts,), jnp.float32, smallest / len(split), high / len(split)))
        gain = gain * jnp.repeat(heights, extent[dim] // parts).reshape([-1 if axis == dim else 1 for axis in range(len(extent))])
    return gain


def gaussian(rng, shape, width, bound, shards=(), kind=jnp.bfloat16):
    entries = width * jax.random.normal(rng, shape, jnp.float32)
    if shards:
        entries = entries * levels(rng, shape, shards, -0.22, 0.18)
    return jnp.clip(entries, -bound, bound).astype(kind)


def noise_with(stream_key, extent, scale, limit, split, heavy, kind=jnp.bfloat16):
    drawn = scale * jax.random.normal(stream_key, extent, jnp.float32)
    if split:
        drawn = drawn * levels(stream_key, extent, split, -0.22, 0.18)
    return jnp.clip(strengthened(drawn, jax.random.fold_in(stream_key, 3), *heavy), -limit, limit).astype(kind)


def setup_inputs(seed: int = 0, part: int = 0) -> dict:
    seeds = jax.random.split(jax.random.key(seed), 5)
    own_keys = jax.random.split(jax.random.fold_in(seeds[4], part), 5)
    amplitudes = gaussian(own_keys[0], (PAIRS, CD), 1.0, 6.0, ((0, 16),))
    integrals = noise_with(own_keys[1], (AB, CD), (CD // 2) ** -0.5, 0.0625, ((1, 16),), (1, 0, 16, 2.0))
    block_mask = plant((jax.random.randint(own_keys[2], (AB_TILES, CD_TILES), 0, 2) < 1).astype(jnp.int32), jax.random.fold_in(own_keys[2], 1), 0, 1)
    pair_list = jax.random.permutation(own_keys[3], PAIRS).astype(jnp.int32)
    return dict(amplitudes=amplitudes, integrals=integrals, block_mask=block_mask, pair_list=pair_list)


def reference(amplitudes, integrals, block_mask, pair_list):
    tiles_ab = block_mask.shape[0]
    tiles_cd = block_mask.shape[1]
    shaped = integrals.reshape(tiles_ab, TILE, tiles_cd, TILE)
    masked = (shaped * block_mask.astype(integrals.dtype)[:, None, :, None]).reshape(integrals.shape)

    def one_block(rows):
        return jnp.dot(rows, amplitudes.T, preferred_element_type=jnp.float32)

    ladder = lax.map(one_block, masked.reshape(tiles_ab, TILE, -1)).reshape(integrals.shape[0], -1)
    residual = jnp.zeros_like(ladder).at[:, pair_list].set(ladder)
    return residual
```

```python
import functools

import jax
import jax.numpy as jnp
from jax import lax
from jax.experimental import pallas as pl
from jax.experimental.pallas import tpu as pltpu
from jax.sharding import PartitionSpec as P

TILE = 128
CHUNKS = 1
WHOLE = pl.BlockSpec(memory_space=pltpu.VMEM)


def f32(*shape):
    return jax.ShapeDtypeStruct(shape, jnp.float32)


def call(kernel, name, outs, *args):
    moved = sum(a.size * a.dtype.itemsize for a in (*args, *outs))
    return pl.pallas_call(
        kernel,
        out_shape=outs,
        in_specs=[WHOLE] * len(args),
        out_specs=[WHOLE] * len(outs),
        name=name,
        compiler_params=pltpu.CompilerParams(vmem_limit_bytes=48 * 2**20),
        cost_estimate=pl.CostEstimate(flops=moved // 4, bytes_accessed=moved, transcendentals=0),
    )(*args)


def product_kernel(me_ref, mask_ref, rows_ref, amplitudes_ref, send_ref, keep_ref):
    step = pl.program_id(0)
    me = me_ref[0]
    tiles_cd = mask_ref.shape[1]
    base = ((me // 2) ^ step) * 2
    for out_ref, core in ((send_ref, 1 - me % 2), (keep_ref, me % 2)):
        rows = rows_ref[pl.ds(pl.multiple_of(core * TILE, TILE), TILE), :]
        masked = jnp.concatenate(
            [
                rows[:, t * TILE : (t + 1) * TILE] * mask_ref[base + core, t].astype(jnp.float32).astype(rows.dtype)
                for t in range(tiles_cd)
            ],
            axis=1,
        )
        out_ref[0] = lax.dot_general(
            masked, amplitudes_ref[...], (((1,), (1,)), ((), ())), preferred_element_type=jnp.float32
        )


def product(me, block_mask, integrals, amplitudes):
    rows, depth = integrals.shape
    pairs = amplitudes.shape[0]
    chips = rows // (2 * TILE)
    spec = pl.BlockSpec((1, TILE, pairs), lambda k, me: (k, 0, 0))
    return pl.pallas_call(
        product_kernel,
        grid_spec=pltpu.PrefetchScalarGridSpec(
            num_scalar_prefetch=1,
            grid=(chips,),
            in_specs=[
                pl.BlockSpec(memory_space=pltpu.SMEM),
                pl.BlockSpec((2 * TILE, depth), lambda k, me: ((me[0] // 2) ^ k, 0)),
                pl.BlockSpec((pairs, depth), lambda k, me: (0, 0)),
            ],
            out_specs=[spec, spec],
        ),
        out_shape=[f32(chips, TILE, pairs)] * 2,
        name="product",
        compiler_params=pltpu.CompilerParams(vmem_limit_bytes=32 * 2**20),
        cost_estimate=pl.CostEstimate(
            flops=2 * rows * depth * pairs,
            bytes_accessed=2 * rows * depth + 2 * pairs * depth + 4 * rows * pairs,
            transcendentals=0,
        ),
    )(me, block_mask, integrals, amplitudes)


def core_kernel(far, keep_ref, got_ref, a_send, a_keep, b_keep, *b_send):
    half = TILE // 2
    for h in range(far):
        for low in range(2):
            k = 2 * h + low
            a_ref = a_send if low else a_keep
            a_ref[h] = keep_ref[k, :half] + got_ref[k, :half]
            b_ref = b_send[h - 1] if h else b_keep
            b_ref[low] = keep_ref[k, half:] + got_ref[k, half:]


def middle_kernel(far, a_keep, a_got, b_keep, *refs):
    b_got, (b_send, b_own, a_own), a_send = refs[: far - 1], refs[far - 1 : far + 2], refs[far + 2 :]
    for h in range(far):
        a_ref = a_send[h - 1] if h else a_own
        a_ref[...] = a_keep[h] + a_got[h]
    for low in range(2):
        total = b_keep[low]
        for got in b_got:
            total += got[low]
        b_ref = b_send if low else b_own
        b_ref[...] = total


def last_kernel(far, chunks, *refs):
    pairs_refs, refs = refs[:chunks], refs[chunks:]
    out_ref = refs[-1]
    half, pairs = TILE // 2, out_ref.shape[1]
    each = 2 + far
    total = None
    for c in range(chunks):
        a_own, b_own, b_got, *a_got = refs[c * each : (c + 1) * each]
        top = a_own[...]
        for got in a_got:
            top += got[...]
        rest = jnp.concatenate([top, b_own[...] + b_got[...]], axis=0)
        places = lax.broadcasted_iota(jnp.int32, (rest.shape[1], pairs), 1)
        chosen = (pairs_refs[c][...] == places).astype(jnp.float32).astype(jnp.bfloat16)
        for _ in range(3):
            part = rest.astype(jnp.bfloat16)
            rest = rest - part.astype(jnp.float32)
            moved = jnp.dot(part, chosen, preferred_element_type=jnp.float32)
            total = moved if total is None else total + moved
    out_ref[...] = total


def per_device(devices, amplitudes, integrals, block_mask, pair_list):
    me = lax.axis_index("ab").reshape(1)
    far = devices // 4
    half = TILE // 2
    mine, depth = amplitudes.shape[0], integrals.shape[1]
    rows = mine // CHUNKS
    pairs = rows * devices

    def swap(value, bits):
        return lax.ppermute(value, "ab", [(i, i ^ bits) for i in range(devices)])

    places, pieces = [], []
    for c in range(CHUNKS):
        places.append(pair_list.reshape(devices, CHUNKS, rows)[:, c].reshape(-1, 1))
        chunk = amplitudes[c * rows : (c + 1) * rows]
        received = lax.all_to_all(chunk, "ab", split_axis=1, concat_axis=0, tiled=True)
        send, keep = product(me, block_mask, integrals, received)
        got = swap(send, 1)
        quarter = f32(far, half, pairs)
        a_send, a_keep, b_keep, *b_send = call(
            functools.partial(core_kernel, far), "core_sum",
            [quarter, quarter] + [f32(2, half, pairs)] * far, keep, got,
        )
        b_got = [swap(b, (h + 1) * 4) for h, b in enumerate(b_send)]
        a_got = swap(a_send, 2)
        b_send, b_own, a_own, *a_send = call(
            functools.partial(middle_kernel, far), "middle_sum",
            [f32(half, pairs)] * (far + 2), a_keep, a_got, b_keep, *b_got,
        )
        a_got = [swap(a, (h + 1) * 4) for h, a in enumerate(a_send)]
        b_got = swap(b_send, 2)
        pieces += [a_own, b_own, b_got, *a_got]
    return call(
        functools.partial(last_kernel, far, CHUNKS), "last_sum",
        [f32(TILE, pair_list.shape[0])], *places, *pieces,
    )[0]


def solution(mesh):
    placed = (P(("groups", "ab"), None), P("groups", "ab"), P("groups", "ab"), P("groups"))
    return jax.shard_map(
        functools.partial(per_device, mesh.shape["ab"]),
        mesh=mesh, in_specs=placed, out_specs=P(("groups", "ab"), None), check_vma=False,
    )
```

```python
import functools

import jax
import jax.numpy as jnp
from jax import lax
from jax.experimental import pallas as pl
from jax.experimental.pallas import tpu as pltpu
from jax.sharding import PartitionSpec as P

TILE = 128
WIRE = jnp.float32
EXTRA = 16


def STREAMS(bits):
    return [(0, TILE // 2, bits), (TILE // 2, TILE, bits[1:] + bits[:1])]


WHOLE = pl.BlockSpec(memory_space=pltpu.VMEM)
SCALARS = pl.BlockSpec(memory_space=pltpu.SMEM)


def call(kernel, name, outs, *args, scalars=0, scratch=(), flops=0):
    moved = sum(a.size * a.dtype.itemsize for a in (*args, *outs))
    return pl.pallas_call(
        kernel,
        out_shape=outs,
        in_specs=[SCALARS] * scalars + [WHOLE] * (len(args) - scalars),
        out_specs=[WHOLE] * len(outs),
        scratch_shapes=list(scratch),
        name=name,
        compiler_params=pltpu.CompilerParams(vmem_limit_bytes=40 * 2**20),
        cost_estimate=pl.CostEstimate(flops=flops, bytes_accessed=moved, transcendentals=0),
    )(*args)


def sort_kernel(me_ref, amplitudes_ref, send_ref, keep_ref):
    chips, _, depth = keep_ref.shape
    chip, core = me_ref[0] // 2, me_ref[0] % 2
    for k in range(chips):
        for out_ref, to in ((send_ref, 1 - core), (keep_ref, core)):
            start = pl.multiple_of(((chip ^ k) * 2 + to) * depth, depth)
            out_ref[k] = amplitudes_ref[:, pl.ds(start, depth)]


def piece_kernel(me_ref, keep_ref, got_ref, *outs):
    mine = keep_ref.shape[1]
    core = me_ref[0] % 2

    def store(first, second):
        for k, out in enumerate(outs):
            out[:mine] = first[k]
            out[mine:] = second[k]

    pl.when(core == 0)(lambda: store(keep_ref, got_ref))
    pl.when(core == 1)(lambda: store(got_ref, keep_ref))


def mask_kernel(me_ref, mask_ref, rows_ref, out_ref):
    k, core = pl.program_id(0), me_ref[0] % 2
    base = ((me_ref[0] // 2) ^ k) * 2
    for slot, own in enumerate((1 - core, core)):
        rows = pl.ds(pl.multiple_of(own * TILE, TILE), TILE)
        for t in range(mask_ref.shape[1]):
            columns = slice(t * TILE, (t + 1) * TILE)
            factor = mask_ref[base + own, t].astype(jnp.float32).astype(out_ref.dtype)
            out_ref[slot, 0, :, columns] = rows_ref[rows, columns] * factor


def masked_rows(me, block_mask, integrals):
    rows, depth = integrals.shape
    chips = rows // (2 * TILE)
    return pl.pallas_call(
        mask_kernel,
        grid_spec=pltpu.PrefetchScalarGridSpec(
            num_scalar_prefetch=1,
            grid=(chips,),
            in_specs=[SCALARS, pl.BlockSpec((2 * TILE, depth), lambda k, me: ((me[0] // 2) ^ k, 0))],
            out_specs=pl.BlockSpec((2, 1, TILE, depth), lambda k, me: (0, k, 0, 0)),
        ),
        out_shape=jax.ShapeDtypeStruct((2, chips, TILE, depth), integrals.dtype),
        name="mask",
        compiler_params=pltpu.CompilerParams(vmem_limit_bytes=16 * 2**20),
        cost_estimate=pl.CostEstimate(flops=rows * depth, bytes_accessed=4 * rows * depth, transcendentals=0),
    )(me, block_mask, integrals)


def product_kernel(me_ref, masked_ref, *refs):
    *pieces, send_ref, keep_ref, all_ref = refs
    mine, depth = pieces[0].shape
    chip = me_ref[0] // 2
    for k, piece in enumerate(pieces):
        all_ref[pl.ds(pl.multiple_of((chip ^ k) * mine, mine), mine), :] = piece[...]
    for slot, out_ref in enumerate((send_ref, keep_ref)):
        rows = masked_ref[slot].reshape(-1, depth)
        out_ref[...] = lax.dot_general(
            rows, all_ref[...], (((1,), (1,)), ((), ())), preferred_element_type=jnp.float32
        ).reshape(out_ref.shape)


def chip_of(index, bits):
    return sum(((index >> (len(bits) - 1 - i)) & 1) << b for i, b in enumerate(bits))


def pack(values, out_ref):
    rows = values[0].shape[0]
    if out_ref.dtype == jnp.float32:
        for i, value in enumerate(values):
            out_ref[i * rows : (i + 1) * rows] = value
        return
    largest = functools.reduce(jnp.maximum, [jnp.max(jnp.abs(v), axis=0, keepdims=True) for v in values])
    exponent = jnp.ceil(jnp.log2(jnp.maximum(largest, 2.0**-110)) + 0.01)
    factor = jnp.exp2(15.0 - exponent)
    for i, value in enumerate(values):
        out_ref[i * rows : (i + 1) * rows] = jnp.round(value * factor).astype(jnp.int32).astype(jnp.int16)
    last = (EXTRA, exponent.shape[1])
    out_ref[len(values) * rows :] = jnp.broadcast_to(exponent, last).astype(jnp.int32).astype(jnp.int16)


def unpack(got_ref, rows):
    if got_ref.dtype == jnp.float32:
        return [got_ref[i : i + rows] for i in range(0, got_ref.shape[0], rows)]
    stop = got_ref.shape[0] - EXTRA
    exponent = got_ref[stop:].astype(jnp.int32).astype(jnp.float32)[:1]
    step = jnp.exp2(exponent - 15.0)
    return [got_ref[i : i + rows].astype(jnp.int32).astype(jnp.float32) * step for i in range(0, stop, rows)]


def packed(blocks, rows, columns):
    if WIRE == jnp.float32:
        return jax.ShapeDtypeStruct((blocks * rows, columns), WIRE)
    return jax.ShapeDtypeStruct((blocks * rows + EXTRA, columns), WIRE)


def first_kernel(streams, keep_ref, got_ref, *outs):
    for (start, stop, bits), send, keep in zip(streams, outs[::2], outs[1::2], strict=True):
        half = keep.shape[0]
        sums = []
        for index in range(2 * half):
            k = chip_of(index, bits)
            sums.append(keep_ref[k, start:stop] + got_ref[k, start:stop])
        for index in range(half):
            keep[index] = sums[index]
        pack(sums[half:], send)


def halve_kernel(keep_ref, got_ref, send, keep):
    half = keep.shape[0]
    got = unpack(got_ref, keep.shape[1])
    for index in range(half):
        keep[index] = keep_ref[index] + got[index]
    pack([keep_ref[index] + got[index] for index in range(half, 2 * half)], send)


def last_kernel(count, place_ref, *refs):
    *sums, out_ref = refs
    parts = [sums[2 * i][0] + unpack(sums[2 * i + 1], sums[2 * i].shape[1])[0] for i in range(count)]
    rest = jnp.concatenate(parts, axis=0) if count > 1 else parts[0]
    columns = lax.broadcasted_iota(jnp.int32, (rest.shape[1], out_ref.shape[1]), 1)
    chosen = (place_ref[...] == columns).astype(jnp.float32).astype(jnp.bfloat16)
    total = None
    for _ in range(3):
        part = rest.astype(jnp.bfloat16)
        rest = rest - part.astype(jnp.float32)
        moved = jnp.dot(part, chosen, preferred_element_type=jnp.float32)
        total = moved if total is None else total + moved
    out_ref[...] = total


def per_device(devices, amplitudes, integrals, block_mask, pair_list):
    me = lax.axis_index("ab").reshape(1)
    chips = devices // 2
    mine, depth = amplitudes.shape[0], integrals.shape[1]
    pairs = mine * devices
    kind = amplitudes.dtype

    def swap(value, bits):
        return lax.ppermute(value, "ab", [(i, i ^ bits) for i in range(devices)])

    block = jax.ShapeDtypeStruct((chips, mine, depth), kind)
    send, keep = call(sort_kernel, "sort", [block] * 2, me, amplitudes, scalars=1)
    got = swap(send, 1)
    piece = jax.ShapeDtypeStruct((2 * mine, depth), kind)
    pieces = call(piece_kernel, "pieces", [piece] * chips, me, keep, got, scalars=1)
    masked = masked_rows(me, block_mask, integrals)
    received = [pieces[0]] + [None] * (chips - 1)
    for k in reversed(range(1, chips)):
        received[k] = swap(pieces[k], 2 * k)

    partial = jax.ShapeDtypeStruct((chips, TILE, pairs), jnp.float32)
    send, keep = call(
        product_kernel, "product", [partial] * 2, me, masked, *received, scalars=1,
        scratch=[pltpu.VMEM((pairs, depth), kind)], flops=4 * chips * TILE * depth * pairs,
    )
    got = swap(send, 1)

    bits = tuple(range((chips - 1).bit_length()))
    streams = STREAMS(bits)
    outs = []
    for start, stop, _ in streams:
        outs += [packed(chips // 2, stop - start, pairs), jax.ShapeDtypeStruct((chips // 2, stop - start, pairs), jnp.float32)]
    state = call(functools.partial(first_kernel, streams), "core_sum", outs, keep, got)
    sums = []
    for s, (start, stop, order) in enumerate(streams):
        send, keep = state[2 * s : 2 * s + 2]
        for step, bit in enumerate(order):
            got = swap(send, 2 << bit)
            if step < len(order) - 1:
                half = keep.shape[0] // 2
                outs = [packed(half, stop - start, pairs), jax.ShapeDtypeStruct((half, stop - start, pairs), jnp.float32)]
                send, keep = call(halve_kernel, "halve", outs, keep, got)
        sums += [keep, got]
    return call(
        functools.partial(last_kernel, len(streams)), "last",
        [jax.ShapeDtypeStruct((TILE, pairs), jnp.float32)], pair_list.reshape(-1, 1), *sums,
    )[0]


def solution(mesh):
    placed = (P(("groups", "ab"), None), P("groups", "ab"), P("groups", "ab"), P("groups"))
    return jax.shard_map(
        functools.partial(per_device, mesh.shape["ab"]),
        mesh=mesh, in_specs=placed, out_specs=P(("groups", "ab"), None), check_vma=False,
    )
```

```python
import functools

import jax
import jax.numpy as jnp
from jax import lax
from jax.experimental import pallas as pl
from jax.experimental.pallas import tpu as pltpu
from jax.sharding import PartitionSpec as P

TILE = 128
WIRE = jnp.int16
EXTRA = 16


def STREAMS(bits):
    return [(0, TILE // 2, bits), (TILE // 2, TILE, bits[1:] + bits[:1])]


WHOLE = pl.BlockSpec(memory_space=pltpu.VMEM)
SCALARS = pl.BlockSpec(memory_space=pltpu.SMEM)


def call(kernel, name, outs, *args, scalars=0, scratch=(), flops=0):
    moved = sum(a.size * a.dtype.itemsize for a in (*args, *outs))
    return pl.pallas_call(
        kernel,
        out_shape=outs,
        in_specs=[SCALARS] * scalars + [WHOLE] * (len(args) - scalars),
        out_specs=[WHOLE] * len(outs),
        scratch_shapes=list(scratch),
        name=name,
        compiler_params=pltpu.CompilerParams(vmem_limit_bytes=40 * 2**20),
        cost_estimate=pl.CostEstimate(flops=flops, bytes_accessed=moved, transcendentals=0),
    )(*args)


def sort_kernel(me_ref, amplitudes_ref, send_ref, keep_ref):
    chips, _, depth = keep_ref.shape
    chip, core = me_ref[0] // 2, me_ref[0] % 2
    for k in range(chips):
        for out_ref, to in ((send_ref, 1 - core), (keep_ref, core)):
            start = pl.multiple_of(((chip ^ k) * 2 + to) * depth, depth)
            out_ref[k] = amplitudes_ref[:, pl.ds(start, depth)]


def piece_kernel(me_ref, keep_ref, got_ref, *outs):
    mine = keep_ref.shape[1]
    core = me_ref[0] % 2

    def store(first, second):
        for k, out in enumerate(outs):
            out[:mine] = first[k]
            out[mine:] = second[k]

    pl.when(core == 0)(lambda: store(keep_ref, got_ref))
    pl.when(core == 1)(lambda: store(got_ref, keep_ref))


def mask_kernel(me_ref, mask_ref, rows_ref, out_ref):
    k, core = pl.program_id(0), me_ref[0] % 2
    base = ((me_ref[0] // 2) ^ k) * 2
    for slot, own in enumerate((1 - core, core)):
        rows = pl.ds(pl.multiple_of(own * TILE, TILE), TILE)
        for t in range(mask_ref.shape[1]):
            columns = slice(t * TILE, (t + 1) * TILE)
            factor = mask_ref[base + own, t].astype(jnp.float32).astype(out_ref.dtype)
            out_ref[slot, 0, :, columns] = rows_ref[rows, columns] * factor


def masked_rows(me, block_mask, integrals):
    rows, depth = integrals.shape
    chips = rows // (2 * TILE)
    return pl.pallas_call(
        mask_kernel,
        grid_spec=pltpu.PrefetchScalarGridSpec(
            num_scalar_prefetch=1,
            grid=(chips,),
            in_specs=[SCALARS, pl.BlockSpec((2 * TILE, depth), lambda k, me: ((me[0] // 2) ^ k, 0))],
            out_specs=pl.BlockSpec((2, 1, TILE, depth), lambda k, me: (0, k, 0, 0)),
        ),
        out_shape=jax.ShapeDtypeStruct((2, chips, TILE, depth), integrals.dtype),
        name="mask",
        compiler_params=pltpu.CompilerParams(vmem_limit_bytes=16 * 2**20),
        cost_estimate=pl.CostEstimate(flops=rows * depth, bytes_accessed=4 * rows * depth, transcendentals=0),
    )(me, block_mask, integrals)


def product_kernel(me_ref, masked_ref, *refs):
    *pieces, send_ref, keep_ref, all_ref = refs
    mine, depth = pieces[0].shape
    chip = me_ref[0] // 2
    for k, piece in enumerate(pieces):
        all_ref[pl.ds(pl.multiple_of((chip ^ k) * mine, mine), mine), :] = piece[...]
    for slot, out_ref in enumerate((send_ref, keep_ref)):
        rows = masked_ref[slot].reshape(-1, depth)
        out_ref[...] = lax.dot_general(
            rows, all_ref[...], (((1,), (1,)), ((), ())), preferred_element_type=jnp.float32
        ).reshape(out_ref.shape)


def chip_of(index, bits):
    return sum(((index >> (len(bits) - 1 - i)) & 1) << b for i, b in enumerate(bits))


def pack(values, out_ref):
    rows = values[0].shape[0]
    if out_ref.dtype == jnp.float32:
        for i, value in enumerate(values):
            out_ref[i * rows : (i + 1) * rows] = value
        return
    largest = functools.reduce(jnp.maximum, [jnp.max(jnp.abs(v), axis=0, keepdims=True) for v in values])
    exponent = jnp.ceil(jnp.log2(jnp.maximum(largest, 2.0**-110)) + 0.01)
    factor = jnp.exp2(15.0 - exponent)
    for i, value in enumerate(values):
        out_ref[i * rows : (i + 1) * rows] = jnp.round(value * factor).astype(jnp.int32).astype(jnp.int16)
    last = (EXTRA, exponent.shape[1])
    out_ref[len(values) * rows :] = jnp.broadcast_to(exponent, last).astype(jnp.int32).astype(jnp.int16)


def unpack(got_ref, rows):
    if got_ref.dtype == jnp.float32:
        return [got_ref[i : i + rows] for i in range(0, got_ref.shape[0], rows)]
    stop = got_ref.shape[0] - EXTRA
    exponent = got_ref[stop:].astype(jnp.int32).astype(jnp.float32)[:1]
    step = jnp.exp2(exponent - 15.0)
    return [got_ref[i : i + rows].astype(jnp.int32).astype(jnp.float32) * step for i in range(0, stop, rows)]


def packed(blocks, rows, columns):
    if WIRE == jnp.float32:
        return jax.ShapeDtypeStruct((blocks * rows, columns), WIRE)
    return jax.ShapeDtypeStruct((blocks * rows + EXTRA, columns), WIRE)


def first_kernel(streams, keep_ref, got_ref, *outs):
    for (start, stop, bits), send, keep in zip(streams, outs[::2], outs[1::2], strict=True):
        half = keep.shape[0]
        sums = []
        for index in range(2 * half):
            k = chip_of(index, bits)
            sums.append(keep_ref[k, start:stop] + got_ref[k, start:stop])
        for index in range(half):
            keep[index] = sums[index]
        pack(sums[half:], send)


def halve_kernel(keep_ref, got_ref, send, keep):
    half = keep.shape[0]
    got = unpack(got_ref, keep.shape[1])
    for index in range(half):
        keep[index] = keep_ref[index] + got[index]
    pack([keep_ref[index] + got[index] for index in range(half, 2 * half)], send)


def last_kernel(count, place_ref, *refs):
    *sums, out_ref = refs
    parts = [sums[2 * i][0] + unpack(sums[2 * i + 1], sums[2 * i].shape[1])[0] for i in range(count)]
    rest = jnp.concatenate(parts, axis=0) if count > 1 else parts[0]
    columns = lax.broadcasted_iota(jnp.int32, (rest.shape[1], out_ref.shape[1]), 1)
    chosen = (place_ref[...] == columns).astype(jnp.float32).astype(jnp.bfloat16)
    total = None
    for _ in range(3):
        part = rest.astype(jnp.bfloat16)
        rest = rest - part.astype(jnp.float32)
        moved = jnp.dot(part, chosen, preferred_element_type=jnp.float32)
        total = moved if total is None else total + moved
    out_ref[...] = total


def per_device(devices, amplitudes, integrals, block_mask, pair_list):
    me = lax.axis_index("ab").reshape(1)
    chips = devices // 2
    mine, depth = amplitudes.shape[0], integrals.shape[1]
    pairs = mine * devices
    kind = amplitudes.dtype

    def swap(value, bits):
        return lax.ppermute(value, "ab", [(i, i ^ bits) for i in range(devices)])

    block = jax.ShapeDtypeStruct((chips, mine, depth), kind)
    send, keep = call(sort_kernel, "sort", [block] * 2, me, amplitudes, scalars=1)
    got = swap(send, 1)
    piece = jax.ShapeDtypeStruct((2 * mine, depth), kind)
    pieces = call(piece_kernel, "pieces", [piece] * chips, me, keep, got, scalars=1)
    masked = masked_rows(me, block_mask, integrals)
    received = [pieces[0]] + [None] * (chips - 1)
    for k in reversed(range(1, chips)):
        received[k] = swap(pieces[k], 2 * k)

    partial = jax.ShapeDtypeStruct((chips, TILE, pairs), jnp.float32)
    send, keep = call(
        product_kernel, "product", [partial] * 2, me, masked, *received, scalars=1,
        scratch=[pltpu.VMEM((pairs, depth), kind)], flops=4 * chips * TILE * depth * pairs,
    )
    got = swap(send, 1)

    bits = tuple(range((chips - 1).bit_length()))
    streams = STREAMS(bits)
    outs = []
    for start, stop, _ in streams:
        outs += [packed(chips // 2, stop - start, pairs), jax.ShapeDtypeStruct((chips // 2, stop - start, pairs), jnp.float32)]
    state = call(functools.partial(first_kernel, streams), "core_sum", outs, keep, got)
    sums = []
    for s, (start, stop, order) in enumerate(streams):
        send, keep = state[2 * s : 2 * s + 2]
        for step, bit in enumerate(order):
            got = swap(send, 2 << bit)
            if step < len(order) - 1:
                half = keep.shape[0] // 2
                outs = [packed(half, stop - start, pairs), jax.ShapeDtypeStruct((half, stop - start, pairs), jnp.float32)]
                send, keep = call(halve_kernel, "halve", outs, keep, got)
        sums += [keep, got]
    return call(
        functools.partial(last_kernel, len(streams)), "last",
        [jax.ShapeDtypeStruct((TILE, pairs), jnp.float32)], pair_list.reshape(-1, 1), *sums,
    )[0]


def solution(mesh):
    placed = (P(("groups", "ab"), None), P("groups", "ab"), P("groups", "ab"), P("groups"))
    return jax.shard_map(
        functools.partial(per_device, mesh.shape["ab"]),
        mesh=mesh, in_specs=placed, out_specs=P(("groups", "ab"), None), check_vma=False,
    )
```

```python
import functools

import jax
import jax.numpy as jnp
from jax import lax
from jax.experimental import pallas as pl
from jax.experimental.pallas import tpu as pltpu
from jax.sharding import PartitionSpec as P

TILE = 128
EXTRA = 16


def sending(chips):
    return [chips - 1] + list(range(1, chips // 2)) + list(reversed(range(chips // 2, chips - 1)))


WHOLE = pl.BlockSpec(memory_space=pltpu.VMEM)
SCALARS = pl.BlockSpec(memory_space=pltpu.SMEM)


def call(kernel, name, outs, *args, scalars=0, scratch=(), flops=0):
    moved = sum(a.size * a.dtype.itemsize for a in (*args, *outs))
    return pl.pallas_call(
        kernel,
        out_shape=outs,
        in_specs=[SCALARS] * scalars + [WHOLE] * (len(args) - scalars),
        out_specs=[WHOLE] * len(outs),
        scratch_shapes=list(scratch),
        name=name,
        compiler_params=pltpu.CompilerParams(vmem_limit_bytes=40 * 2**20),
        cost_estimate=pl.CostEstimate(flops=flops, bytes_accessed=moved, transcendentals=0),
    )(*args)


def sort_kernel(me_ref, amplitudes_ref, send_ref, keep_ref):
    chips, _, depth = keep_ref.shape
    chip, core = me_ref[0] // 2, me_ref[0] % 2
    for k in range(chips):
        for out_ref, to in ((send_ref, 1 - core), (keep_ref, core)):
            start = pl.multiple_of(((chip ^ k) * 2 + to) * depth, depth)
            out_ref[k] = amplitudes_ref[:, pl.ds(start, depth)]


def piece_kernel(me_ref, keep_ref, got_ref, *outs):
    mine = keep_ref.shape[1]
    core = me_ref[0] % 2

    def store(first, second):
        for k, out in enumerate(outs):
            out[:mine] = first[k]
            out[mine:] = second[k]

    pl.when(core == 0)(lambda: store(keep_ref, got_ref))
    pl.when(core == 1)(lambda: store(got_ref, keep_ref))


def mask_kernel(me_ref, mask_ref, rows_ref, out_ref):
    k, core = pl.program_id(0), me_ref[0] % 2
    base = ((me_ref[0] // 2) ^ k) * 2
    for slot, own in enumerate((1 - core, core)):
        rows = pl.ds(pl.multiple_of(own * TILE, TILE), TILE)
        for t in range(mask_ref.shape[1]):
            columns = slice(t * TILE, (t + 1) * TILE)
            factor = mask_ref[base + own, t].astype(jnp.float32).astype(out_ref.dtype)
            out_ref[slot, 0, :, columns] = rows_ref[rows, columns] * factor


def masked_rows(me, block_mask, integrals):
    rows, depth = integrals.shape
    chips = rows // (2 * TILE)
    return pl.pallas_call(
        mask_kernel,
        grid_spec=pltpu.PrefetchScalarGridSpec(
            num_scalar_prefetch=1,
            grid=(chips,),
            in_specs=[SCALARS, pl.BlockSpec((2 * TILE, depth), lambda k, me: ((me[0] // 2) ^ k, 0))],
            out_specs=pl.BlockSpec((2, 1, TILE, depth), lambda k, me: (0, k, 0, 0)),
        ),
        out_shape=jax.ShapeDtypeStruct((2, chips, TILE, depth), integrals.dtype),
        name="mask",
        compiler_params=pltpu.CompilerParams(vmem_limit_bytes=16 * 2**20),
        cost_estimate=pl.CostEstimate(flops=rows * depth, bytes_accessed=4 * rows * depth, transcendentals=0),
    )(me, block_mask, integrals)


def product_kernel(me_ref, masked_ref, *refs):
    *pieces, send_ref, keep_ref, all_ref = refs
    mine, depth = pieces[0].shape
    chip = me_ref[0] // 2 % len(pieces)
    for k, piece in enumerate(pieces):
        all_ref[pl.ds(pl.multiple_of((chip ^ k) * mine, mine), mine), :] = piece[...]
    for slot, out_ref in enumerate((send_ref, keep_ref)):
        rows = masked_ref[slot].reshape(-1, depth)
        out_ref[...] = lax.dot_general(
            rows, all_ref[...], (((1,), (1,)), ((), ())), preferred_element_type=jnp.float32
        ).reshape(out_ref.shape)


def chip_of(index, bits):
    return sum(((index >> (len(bits) - 1 - i)) & 1) << b for i, b in enumerate(bits))


def pack(values, out_ref):
    rows = values[0].shape[0]
    largest = functools.reduce(jnp.maximum, [jnp.max(jnp.abs(v), axis=0, keepdims=True) for v in values])
    exponent = jnp.ceil(jnp.log2(jnp.maximum(largest, 2.0**-110)) + 0.01)
    factor = jnp.exp2(15.0 - exponent)
    for i, value in enumerate(values):
        out_ref[i * rows : (i + 1) * rows] = jnp.round(value * factor).astype(jnp.int32).astype(jnp.int16)
    last = (EXTRA, exponent.shape[1])
    out_ref[len(values) * rows :] = jnp.broadcast_to(exponent, last).astype(jnp.int32).astype(jnp.int16)


def unpack(got_ref):
    stop = got_ref.shape[0] - EXTRA
    exponent = got_ref[stop:].astype(jnp.int32).astype(jnp.float32)[:1]
    step = jnp.exp2(exponent - 15.0)
    return [got_ref[i : i + TILE].astype(jnp.int32).astype(jnp.float32) * step for i in range(0, stop, TILE)]


def packed(blocks, columns):
    return jax.ShapeDtypeStruct((blocks * TILE + EXTRA, columns), jnp.int16)


def plain(blocks, columns):
    return jax.ShapeDtypeStruct((blocks, TILE, columns), jnp.float32)


def first_kernel(bits, keep_ref, got_ref, send, keep):
    half = keep.shape[0]
    sums = []
    for index in range(2 * half):
        k = chip_of(index, bits)
        sums.append(keep_ref[k] + got_ref[k])
    for index in range(half):
        keep[index] = sums[index]
    pack(sums[half:], send)


def halve_kernel(keep_ref, got_ref, send, keep):
    half = keep.shape[0]
    got = unpack(got_ref)
    for index in range(half):
        keep[index] = keep_ref[index] + got[index]
    pack([keep_ref[index] + got[index] for index in range(half, 2 * half)], send)


def join_kernel(near_keep, near_got, far_keep, far_got, send, keep):
    both = []
    for c, (kept, got) in enumerate(((near_keep, near_got), (far_keep, far_got))):
        mine, theirs = unpack(got)
        keep[c] = kept[0] + mine
        both.append(kept[1] + theirs)
    pack([jnp.concatenate(both, axis=1)], send)


def last_kernel(half, me_ref, keep_ref, got_ref, places_ref, out_ref):
    pairs = keep_ref.shape[2]
    high = (me_ref[0] >= half).astype(jnp.int32)
    got = unpack(got_ref)[0]
    total = None
    for c in range(2):
        rest = keep_ref[c] + got[:, (1 - c) * pairs : (2 - c) * pairs]
        place = jnp.where(high == c, places_ref[:pairs], places_ref[pairs:])
        columns = lax.broadcasted_iota(jnp.int32, (pairs, out_ref.shape[1]), 1)
        chosen = (place == columns).astype(jnp.float32).astype(jnp.bfloat16)
        for _ in range(3):
            part = rest.astype(jnp.bfloat16)
            rest = rest - part.astype(jnp.float32)
            moved = jnp.dot(part, chosen, preferred_element_type=jnp.float32)
            total = moved if total is None else total + moved
    out_ref[...] = total


def per_device(devices, amplitudes, integrals, block_mask, pair_list):
    me = lax.axis_index("ab").reshape(1)
    chips = devices // 2
    mine, depth = amplitudes.shape[0], integrals.shape[1]
    pairs = mine * chips
    kind = amplitudes.dtype

    def swap(value, bits):
        return lax.ppermute(value, "ab", [(i, i ^ bits) for i in range(devices)])

    block = jax.ShapeDtypeStruct((chips, mine, depth), kind)
    send, keep = call(sort_kernel, "sort", [block] * 2, me, amplitudes, scalars=1)
    got = swap(send, 1)
    piece = jax.ShapeDtypeStruct((2 * mine, depth), kind)
    pieces = call(piece_kernel, "pieces", [piece] * chips, me, keep, got, scalars=1)
    received = {0: pieces[0]}
    for k in sending(chips):
        received[k] = swap(pieces[k], 2 * k)
    masked = masked_rows(me, block_mask, integrals)

    half = chips // 2
    bits = tuple(range((chips - 1).bit_length()))
    sums = []
    for first in (0, half):
        send, keep = call(
            product_kernel, "product", [plain(chips, pairs)] * 2, me, masked,
            *[received[k] for k in range(first, first + half)], scalars=1,
            scratch=[pltpu.VMEM((pairs, depth), kind)], flops=4 * chips * TILE * depth * pairs,
        )
        got = swap(send, 1)
        blocks = half
        send, keep = call(
            functools.partial(first_kernel, bits), "core_sum", [packed(blocks, pairs), plain(blocks, pairs)], keep, got
        )
        for bit in bits[:-1]:
            got = swap(send, 2 << bit)
            if bit < bits[-2]:
                blocks //= 2
                send, keep = call(halve_kernel, "halve", [packed(blocks, pairs), plain(blocks, pairs)], keep, got)
        sums += [keep, got]
    send, keep = call(join_kernel, "join", [packed(1, 2 * pairs), plain(2, pairs)], *sums)
    got = swap(send, 2 << bits[-1])
    return call(
        functools.partial(last_kernel, chips), "last", [jax.ShapeDtypeStruct((TILE, 2 * pairs), jnp.float32)],
        me, keep, got, pair_list.reshape(-1, 1), scalars=1,
    )[0]


def solution(mesh):
    placed = (P(("groups", "ab"), None), P("groups", "ab"), P("groups", "ab"), P("groups"))
    return jax.shard_map(
        functools.partial(per_device, mesh.shape["ab"]),
        mesh=mesh, in_specs=placed, out_specs=P(("groups", "ab"), None), check_vma=False,
    )
```

```python
import functools

import jax
import jax.numpy as jnp
from jax import lax
from jax.experimental import pallas as pl
from jax.experimental.pallas import tpu as pltpu
from jax.sharding import PartitionSpec as P

TILE = 128
EXTRA = 16


def sending(chips):
    return [chips - 1] + list(range(1, chips // 2)) + list(reversed(range(chips // 2, chips - 1)))


WHOLE = pl.BlockSpec(memory_space=pltpu.VMEM)
SCALARS = pl.BlockSpec(memory_space=pltpu.SMEM)


def call(kernel, name, outs, *args, scalars=0, scratch=(), flops=0):
    moved = sum(a.size * a.dtype.itemsize for a in (*args, *outs))
    return pl.pallas_call(
        kernel,
        out_shape=outs,
        in_specs=[SCALARS] * scalars + [WHOLE] * (len(args) - scalars),
        out_specs=[WHOLE] * len(outs),
        scratch_shapes=list(scratch),
        name=name,
        compiler_params=pltpu.CompilerParams(vmem_limit_bytes=40 * 2**20),
        cost_estimate=pl.CostEstimate(flops=flops, bytes_accessed=moved, transcendentals=0),
    )(*args)


def sort_kernel(me_ref, amplitudes_ref, send_ref, keep_ref):
    chips, _, depth = keep_ref.shape
    chip, core = me_ref[0] // 2, me_ref[0] % 2
    for k in range(chips):
        for out_ref, to in ((send_ref, 1 - core), (keep_ref, core)):
            start = pl.multiple_of(((chip ^ k) * 2 + to) * depth, depth)
            out_ref[k] = amplitudes_ref[:, pl.ds(start, depth)]


def piece_kernel(me_ref, keep_ref, got_ref, *outs):
    mine = keep_ref.shape[1]
    core = me_ref[0] % 2

    def store(first, second):
        for k, out in enumerate(outs):
            out[:mine] = first[k]
            out[mine:] = second[k]

    pl.when(core == 0)(lambda: store(keep_ref, got_ref))
    pl.when(core == 1)(lambda: store(got_ref, keep_ref))


def mask_kernel(me_ref, mask_ref, rows_ref, out_ref, block_ref, arrived):
    chips, _, depth = block_ref.shape
    chip, core = me_ref[0] // 2, me_ref[0] % 2

    def copy(k):
        start = pl.multiple_of((chip ^ k) * (2 * TILE), 2 * TILE)
        return pltpu.make_async_copy(rows_ref.at[pl.ds(start, 2 * TILE), :], block_ref.at[k], arrived.at[k])

    for k in range(chips):
        copy(k).start()

    @pl.loop(0, chips)
    def _(k):
        copy(k).wait()
        for slot, own in enumerate((1 - core, core)):
            rows = pl.ds(pl.multiple_of(own * TILE, TILE), TILE)
            for t in range(mask_ref.shape[1]):
                columns = slice(t * TILE, (t + 1) * TILE)
                factor = mask_ref[(chip ^ k) * 2 + own, t].astype(jnp.float32).astype(out_ref.dtype)
                out_ref[slot, k, :, columns] = block_ref[k, rows, columns] * factor


def masked_rows(me, block_mask, integrals):
    rows, depth = integrals.shape
    chips = rows // (2 * TILE)
    return pl.pallas_call(
        mask_kernel,
        in_specs=[SCALARS, SCALARS, pl.BlockSpec(memory_space=pltpu.HBM)],
        out_specs=WHOLE,
        out_shape=jax.ShapeDtypeStruct((2, chips, TILE, depth), integrals.dtype),
        scratch_shapes=[pltpu.VMEM((chips, 2 * TILE, depth), integrals.dtype), pltpu.SemaphoreType.DMA((chips,))],
        name="mask",
        compiler_params=pltpu.CompilerParams(vmem_limit_bytes=40 * 2**20),
        cost_estimate=pl.CostEstimate(flops=rows * depth, bytes_accessed=4 * rows * depth, transcendentals=0),
    )(me, block_mask, integrals)


def product_kernel(me_ref, masked_ref, *refs):
    *pieces, send_ref, keep_ref, all_ref = refs
    mine, depth = pieces[0].shape
    chip = me_ref[0] // 2 % len(pieces)
    for k, piece in enumerate(pieces):
        all_ref[pl.ds(pl.multiple_of((chip ^ k) * mine, mine), mine), :] = piece[...]
    for slot, out_ref in enumerate((send_ref, keep_ref)):
        rows = masked_ref[slot].reshape(-1, depth)
        out_ref[...] = lax.dot_general(
            rows, all_ref[...], (((1,), (1,)), ((), ())), preferred_element_type=jnp.float32
        ).reshape(out_ref.shape)


def chip_of(index, bits):
    return sum(((index >> (len(bits) - 1 - i)) & 1) << b for i, b in enumerate(bits))


def pack(values, out_ref):
    rows = values[0].shape[0]
    largest = functools.reduce(jnp.maximum, [jnp.max(jnp.abs(v), axis=0, keepdims=True) for v in values])
    exponent = jnp.ceil(jnp.log2(jnp.maximum(largest, 2.0**-110)) + 0.01)
    factor = jnp.exp2(15.0 - exponent)
    for i, value in enumerate(values):
        out_ref[i * rows : (i + 1) * rows] = jnp.round(value * factor).astype(jnp.int32).astype(jnp.int16)
    last = (EXTRA, exponent.shape[1])
    out_ref[len(values) * rows :] = jnp.broadcast_to(exponent, last).astype(jnp.int32).astype(jnp.int16)


def unpack(got_ref):
    stop = got_ref.shape[0] - EXTRA
    exponent = got_ref[stop:].astype(jnp.int32).astype(jnp.float32)[:1]
    step = jnp.exp2(exponent - 15.0)
    return [got_ref[i : i + TILE].astype(jnp.int32).astype(jnp.float32) * step for i in range(0, stop, TILE)]


def packed(blocks, columns):
    return jax.ShapeDtypeStruct((blocks * TILE + EXTRA, columns), jnp.int16)


def plain(blocks, columns):
    return jax.ShapeDtypeStruct((blocks, TILE, columns), jnp.float32)


def first_kernel(bits, keep_ref, got_ref, send, keep):
    half = keep.shape[0]
    sums = []
    for index in range(2 * half):
        k = chip_of(index, bits)
        sums.append(keep_ref[k] + got_ref[k])
    for index in range(half):
        keep[index] = sums[index]
    pack(sums[half:], send)


def halve_kernel(keep_ref, got_ref, send, keep):
    half = keep.shape[0]
    got = unpack(got_ref)
    for index in range(half):
        keep[index] = keep_ref[index] + got[index]
    pack([keep_ref[index] + got[index] for index in range(half, 2 * half)], send)


def join_kernel(near_keep, near_got, far_keep, far_got, send, keep):
    both = []
    for c, (kept, got) in enumerate(((near_keep, near_got), (far_keep, far_got))):
        mine, theirs = unpack(got)
        keep[c] = kept[0] + mine
        both.append(kept[1] + theirs)
    pack([jnp.concatenate(both, axis=1)], send)


def last_kernel(half, me_ref, keep_ref, got_ref, places_ref, out_ref):
    pairs = keep_ref.shape[2]
    high = (me_ref[0] >= half).astype(jnp.int32)
    got = unpack(got_ref)[0]
    total = None
    for c in range(2):
        rest = keep_ref[c] + got[:, (1 - c) * pairs : (2 - c) * pairs]
        place = jnp.where(high == c, places_ref[:pairs], places_ref[pairs:])
        columns = lax.broadcasted_iota(jnp.int32, (pairs, out_ref.shape[1]), 1)
        chosen = (place == columns).astype(jnp.float32).astype(jnp.bfloat16)
        for _ in range(3):
            part = rest.astype(jnp.bfloat16)
            rest = rest - part.astype(jnp.float32)
            moved = jnp.dot(part, chosen, preferred_element_type=jnp.float32)
            total = moved if total is None else total + moved
    out_ref[...] = total


def per_device(devices, amplitudes, integrals, block_mask, pair_list):
    me = lax.axis_index("ab").reshape(1)
    chips = devices // 2
    mine, depth = amplitudes.shape[0], integrals.shape[1]
    pairs = mine * chips
    kind = amplitudes.dtype

    def swap(value, bits):
        return lax.ppermute(value, "ab", [(i, i ^ bits) for i in range(devices)])

    block = jax.ShapeDtypeStruct((chips, mine, depth), kind)
    send, keep = call(sort_kernel, "sort", [block] * 2, me, amplitudes, scalars=1)
    got = swap(send, 1)
    piece = jax.ShapeDtypeStruct((2 * mine, depth), kind)
    pieces = call(piece_kernel, "pieces", [piece] * chips, me, keep, got, scalars=1)
    received = {0: pieces[0]}
    for k in sending(chips):
        received[k] = swap(pieces[k], 2 * k)
    begun = lax.optimization_barrier((me, received[chips - 1]))[0]
    masked = masked_rows(begun, block_mask, integrals)

    half = chips // 2
    bits = tuple(range((chips - 1).bit_length()))

    sums = []
    for first in (0, half):
        send, keep = call(
            product_kernel, "product", [plain(chips, pairs)] * 2, me, masked,
            *[received[k] for k in range(first, first + half)], scalars=1,
            scratch=[pltpu.VMEM((pairs, depth), kind)],
        )
        got = swap(send, 1)
        blocks = half
        send, keep = call(
            functools.partial(first_kernel, bits), "core_sum", [packed(blocks, pairs), plain(blocks, pairs)],
            keep, got,
        )
        for bit in bits[:-1]:
            got = swap(send, 2 << bit)
            if bit < bits[-2]:
                blocks //= 2
                send, keep = call(
                    halve_kernel, "halve", [packed(blocks, pairs), plain(blocks, pairs)],
                    keep, got,
                )
        sums += [keep, got]
    send, keep = call(join_kernel, "join", [packed(1, 2 * pairs), plain(2, pairs)], *sums)
    got = swap(send, 2 << bits[-1])
    return call(
        functools.partial(last_kernel, chips), "last", [jax.ShapeDtypeStruct((TILE, 2 * pairs), jnp.float32)],
        me, keep, got, pair_list.reshape(-1, 1), scalars=1,
    )[0]


def solution(mesh):
    placed = (P(("groups", "ab"), None), P("groups", "ab"), P("groups", "ab"), P("groups"))
    return jax.shard_map(
        functools.partial(per_device, mesh.shape["ab"]),
        mesh=mesh, in_specs=placed, out_specs=P(("groups", "ab"), None), check_vma=False,
    )
```

```python
import functools

import jax
import jax.numpy as jnp
from jax import lax
from jax.experimental import pallas as pl
from jax.experimental.pallas import tpu as pltpu
from jax.sharding import PartitionSpec as P

TILE = 128
EXTRA = 16


def sending(chips):
    return [chips - 1] + list(range(1, chips // 2)) + list(reversed(range(chips // 2, chips - 1)))


WHOLE = pl.BlockSpec(memory_space=pltpu.VMEM)
SCALARS = pl.BlockSpec(memory_space=pltpu.SMEM)


def call(kernel, name, outs, *args, scalars=0, scratch=(), flops=0):
    moved = sum(a.size * a.dtype.itemsize for a in (*args, *outs))
    return pl.pallas_call(
        kernel,
        out_shape=outs,
        in_specs=[SCALARS] * scalars + [WHOLE] * (len(args) - scalars),
        out_specs=[WHOLE] * len(outs),
        scratch_shapes=list(scratch),
        name=name,
        compiler_params=pltpu.CompilerParams(vmem_limit_bytes=40 * 2**20),
        cost_estimate=pl.CostEstimate(flops=flops, bytes_accessed=moved, transcendentals=0),
    )(*args)


def sort_kernel(me_ref, amplitudes_ref, send_ref, keep_ref):
    chips, _, depth = keep_ref.shape
    chip, core = me_ref[0] // 2, me_ref[0] % 2
    for k in range(chips):
        for out_ref, to in ((send_ref, 1 - core), (keep_ref, core)):
            start = pl.multiple_of(((chip ^ k) * 2 + to) * depth, depth)
            out_ref[k] = amplitudes_ref[:, pl.ds(start, depth)]


def piece_kernel(me_ref, keep_ref, got_ref, *outs):
    mine = keep_ref.shape[1]
    core = me_ref[0] % 2

    def store(first, second):
        for k, out in enumerate(outs):
            out[:mine] = first[k]
            out[mine:] = second[k]

    pl.when(core == 0)(lambda: store(keep_ref, got_ref))
    pl.when(core == 1)(lambda: store(got_ref, keep_ref))


def mask_kernel(me_ref, mask_ref, rows_ref, out_ref, block_ref, arrived):
    chips, _, depth = block_ref.shape
    chip, core = me_ref[0] // 2, me_ref[0] % 2

    def copy(k):
        start = pl.multiple_of((chip ^ k) * (2 * TILE), 2 * TILE)
        return pltpu.make_async_copy(rows_ref.at[pl.ds(start, 2 * TILE), :], block_ref.at[k], arrived.at[k])

    for k in range(chips):
        copy(k).start()

    @pl.loop(0, chips)
    def _(k):
        copy(k).wait()
        for slot, own in enumerate((1 - core, core)):
            rows = pl.ds(pl.multiple_of(own * TILE, TILE), TILE)
            for t in range(mask_ref.shape[1]):
                columns = slice(t * TILE, (t + 1) * TILE)
                factor = mask_ref[(chip ^ k) * 2 + own, t].astype(jnp.float32).astype(out_ref.dtype)
                out_ref[slot, k, :, columns] = block_ref[k, rows, columns] * factor


def masked_rows(me, block_mask, integrals):
    rows, depth = integrals.shape
    chips = rows // (2 * TILE)
    return pl.pallas_call(
        mask_kernel,
        in_specs=[SCALARS, SCALARS, pl.BlockSpec(memory_space=pltpu.HBM)],
        out_specs=WHOLE,
        out_shape=jax.ShapeDtypeStruct((2, chips, TILE, depth), integrals.dtype),
        scratch_shapes=[pltpu.VMEM((chips, 2 * TILE, depth), integrals.dtype), pltpu.SemaphoreType.DMA((chips,))],
        name="mask",
        compiler_params=pltpu.CompilerParams(vmem_limit_bytes=40 * 2**20),
        cost_estimate=pl.CostEstimate(flops=rows * depth, bytes_accessed=4 * rows * depth, transcendentals=0),
    )(me, block_mask, integrals)


def product_kernel(me_ref, masked_ref, *refs):
    *pieces, send_ref, keep_ref, all_ref = refs
    mine, depth = pieces[0].shape
    chip = me_ref[0] // 2 % len(pieces)
    for k, piece in enumerate(pieces):
        all_ref[pl.ds(pl.multiple_of((chip ^ k) * mine, mine), mine), :] = piece[...]
    for slot, out_ref in enumerate((send_ref, keep_ref)):
        rows = masked_ref[slot].reshape(-1, depth)
        out_ref[...] = lax.dot_general(
            rows, all_ref[...], (((1,), (1,)), ((), ())), preferred_element_type=jnp.float32
        ).reshape(out_ref.shape)


def chip_of(index, bits):
    return sum(((index >> (len(bits) - 1 - i)) & 1) << b for i, b in enumerate(bits))


def pack(values, out_ref):
    rows = values[0].shape[0]
    largest = functools.reduce(jnp.maximum, [jnp.max(jnp.abs(v), axis=0, keepdims=True) for v in values])
    exponent = jnp.ceil(jnp.log2(jnp.maximum(largest, 2.0**-110)) + 0.01)
    factor = jnp.exp2(15.0 - exponent)
    for i, value in enumerate(values):
        out_ref[i * rows : (i + 1) * rows] = jnp.round(value * factor).astype(jnp.int32).astype(jnp.int16)
    last = (EXTRA, exponent.shape[1])
    out_ref[len(values) * rows :] = jnp.broadcast_to(exponent, last).astype(jnp.int32).astype(jnp.int16)


def unpack(got_ref):
    stop = got_ref.shape[0] - EXTRA
    exponent = got_ref[stop:].astype(jnp.int32).astype(jnp.float32)[:1]
    step = jnp.exp2(exponent - 15.0)
    return [got_ref[i : i + TILE].astype(jnp.int32).astype(jnp.float32) * step for i in range(0, stop, TILE)]


def packed(blocks, columns):
    return jax.ShapeDtypeStruct((blocks * TILE + EXTRA, columns), jnp.int16)


def plain(blocks, columns):
    return jax.ShapeDtypeStruct((blocks, TILE, columns), jnp.float32)


def first_kernel(bits, keep_ref, got_ref, send, keep):
    half = keep.shape[0]
    sums = []
    for index in range(2 * half):
        k = chip_of(index, bits)
        sums.append(keep_ref[k] + got_ref[k])
    for index in range(half):
        keep[index] = sums[index]
    pack(sums[half:], send)


def halve_kernel(keep_ref, got_ref, send, keep):
    half = keep.shape[0]
    got = unpack(got_ref)
    for index in range(half):
        keep[index] = keep_ref[index] + got[index]
    pack([keep_ref[index] + got[index] for index in range(half, 2 * half)], send)


def join_kernel(near_keep, near_got, far_keep, far_got, send, keep):
    both = []
    for c, (kept, got) in enumerate(((near_keep, near_got), (far_keep, far_got))):
        mine, theirs = unpack(got)
        keep[c] = kept[0] + mine
        both.append(kept[1] + theirs)
    pack([jnp.concatenate(both, axis=1)], send)


def place_kernel(chips, me_ref, places_ref, out_ref):
    pairs, columns = places_ref.shape[0] // 2, out_ref.shape[1]
    far = me_ref[0] >= chips
    column = lax.broadcasted_iota(jnp.int32, (pairs, columns), 1)
    low, high = places_ref[:pairs], places_ref[pairs:]
    for c, place in enumerate((jnp.where(far, high, low), jnp.where(far, low, high))):
        ones = (place == column).astype(jnp.float32).astype(out_ref.dtype)
        for part in range(3):
            start = (3 * c + part) * pairs
            out_ref[start : start + pairs] = ones


def last_kernel(keep_ref, got_ref, place_ref, out_ref):
    pairs = keep_ref.shape[2]
    got = unpack(got_ref)[0]
    parts = []
    for c in range(2):
        rest = keep_ref[c] + got[:, (1 - c) * pairs : (2 - c) * pairs]
        for _ in range(3):
            parts.append(rest.astype(jnp.bfloat16))
            rest = rest - parts[-1].astype(jnp.float32)
    out_ref[...] = jnp.dot(jnp.concatenate(parts, axis=1), place_ref[...], preferred_element_type=jnp.float32)


def per_device(devices, amplitudes, integrals, block_mask, pair_list):
    me = lax.axis_index("ab").reshape(1)
    chips = devices // 2
    mine, depth = amplitudes.shape[0], integrals.shape[1]
    pairs = mine * chips
    kind = amplitudes.dtype

    def swap(value, bits):
        return lax.ppermute(value, "ab", [(i, i ^ bits) for i in range(devices)])

    block = jax.ShapeDtypeStruct((chips, mine, depth), kind)
    send, keep = call(sort_kernel, "sort", [block] * 2, me, amplitudes, scalars=1)
    got = swap(send, 1)
    piece = jax.ShapeDtypeStruct((2 * mine, depth), kind)
    pieces = call(piece_kernel, "pieces", [piece] * chips, me, keep, got, scalars=1)
    received = {0: pieces[0]}
    for k in sending(chips):
        received[k] = swap(pieces[k], 2 * k)
    begun = lax.optimization_barrier((me, received[chips - 1]))[0]
    masked = masked_rows(begun, block_mask, integrals)

    place = call(
        functools.partial(place_kernel, chips), "place", [jax.ShapeDtypeStruct((6 * pairs, 2 * pairs), kind)],
        begun, pair_list.reshape(-1, 1), scalars=1,
    )[0]

    half = chips // 2
    bits = tuple(range((chips - 1).bit_length()))

    sums = []
    for first, order in ((0, bits), (half, bits[-2::-1] + bits[-1:])):
        send, keep = call(
            product_kernel, "product", [plain(chips, pairs)] * 2, me, masked,
            *[received[k] for k in range(first, first + half)], scalars=1,
            scratch=[pltpu.VMEM((pairs, depth), kind)],
        )
        got = swap(send, 1)
        blocks = half
        send, keep = call(
            functools.partial(first_kernel, order), "core_sum", [packed(blocks, pairs), plain(blocks, pairs)],
            keep, got,
        )
        for bit in order[:-1]:
            got = swap(send, 2 << bit)
            if blocks > 2:
                blocks //= 2
                send, keep = call(
                    halve_kernel, "halve", [packed(blocks, pairs), plain(blocks, pairs)],
                    keep, got,
                )
        sums += [keep, got]
    send, keep = call(join_kernel, "join", [packed(1, 2 * pairs), plain(2, pairs)], *sums)
    got = swap(send, 2 << bits[-1])
    return call(last_kernel, "last", [jax.ShapeDtypeStruct((TILE, 2 * pairs), jnp.float32)], keep, got, place)[0]


def solution(mesh):
    placed = (P(("groups", "ab"), None), P("groups", "ab"), P("groups", "ab"), P("groups"))
    return jax.shard_map(
        functools.partial(per_device, mesh.shape["ab"]),
        mesh=mesh, in_specs=placed, out_specs=P(("groups", "ab"), None), check_vma=False,
    )
```

```python
import functools

import jax
import jax.numpy as jnp
from jax import lax
from jax.experimental import pallas as pl
from jax.experimental.pallas import tpu as pltpu
from jax.sharding import PartitionSpec as P

TILE = 128
EXTRA = 16


def sending(chips):
    return [chips - 1] + list(range(1, chips // 2)) + list(reversed(range(chips // 2, chips - 1)))


WHOLE = pl.BlockSpec(memory_space=pltpu.VMEM)
SCALARS = pl.BlockSpec(memory_space=pltpu.SMEM)


def call(kernel, name, outs, *args, scalars=0, scratch=(), flops=0):
    moved = sum(a.size * a.dtype.itemsize for a in (*args, *outs))
    return pl.pallas_call(
        kernel,
        out_shape=outs,
        in_specs=[SCALARS] * scalars + [WHOLE] * (len(args) - scalars),
        out_specs=[WHOLE] * len(outs),
        scratch_shapes=list(scratch),
        name=name,
        compiler_params=pltpu.CompilerParams(vmem_limit_bytes=40 * 2**20),
        cost_estimate=pl.CostEstimate(flops=flops, bytes_accessed=moved, transcendentals=0),
    )(*args)


def sort_kernel(me_ref, amplitudes_ref, send_ref, keep_ref):
    chips, _, depth = keep_ref.shape
    chip, core = me_ref[0] // 2, me_ref[0] % 2
    for k in range(chips):
        for out_ref, to in ((send_ref, 1 - core), (keep_ref, core)):
            start = pl.multiple_of(((chip ^ k) * 2 + to) * depth, depth)
            out_ref[k] = amplitudes_ref[:, pl.ds(start, depth)]


def piece_kernel(me_ref, keep_ref, got_ref, *outs):
    mine = keep_ref.shape[1]
    core = me_ref[0] % 2

    def store(first, second):
        for k, out in enumerate(outs):
            out[:mine] = first[k]
            out[mine:] = second[k]

    pl.when(core == 0)(lambda: store(keep_ref, got_ref))
    pl.when(core == 1)(lambda: store(got_ref, keep_ref))


def mask_kernel(me_ref, mask_ref, rows_ref, out_ref, block_ref, arrived):
    chips, _, depth = block_ref.shape
    chip, core = me_ref[0] // 2, me_ref[0] % 2

    def copy(k):
        start = pl.multiple_of((chip ^ k) * (2 * TILE), 2 * TILE)
        return pltpu.make_async_copy(rows_ref.at[pl.ds(start, 2 * TILE), :], block_ref.at[k], arrived.at[k])

    for k in range(chips):
        copy(k).start()

    @pl.loop(0, chips)
    def _(k):
        copy(k).wait()
        for slot, own in enumerate((1 - core, core)):
            rows = pl.ds(pl.multiple_of(own * TILE, TILE), TILE)
            for t in range(mask_ref.shape[1]):
                columns = slice(t * TILE, (t + 1) * TILE)
                factor = mask_ref[(chip ^ k) * 2 + own, t].astype(jnp.float32).astype(out_ref.dtype)
                out_ref[slot, k, :, columns] = block_ref[k, rows, columns] * factor


def masked_rows(me, block_mask, integrals):
    rows, depth = integrals.shape
    chips = rows // (2 * TILE)
    return pl.pallas_call(
        mask_kernel,
        in_specs=[SCALARS, SCALARS, pl.BlockSpec(memory_space=pltpu.HBM)],
        out_specs=WHOLE,
        out_shape=jax.ShapeDtypeStruct((2, chips, TILE, depth), integrals.dtype),
        scratch_shapes=[pltpu.VMEM((chips, 2 * TILE, depth), integrals.dtype), pltpu.SemaphoreType.DMA((chips,))],
        name="mask",
        compiler_params=pltpu.CompilerParams(vmem_limit_bytes=40 * 2**20),
        cost_estimate=pl.CostEstimate(flops=rows * depth, bytes_accessed=4 * rows * depth, transcendentals=0),
    )(me, block_mask, integrals)


def product_kernel(slot, me_ref, masked_ref, *refs):
    *pieces, out_ref, all_ref = refs
    mine, depth = pieces[0].shape
    chip = me_ref[0] // 2 % len(pieces)
    for k, piece in enumerate(pieces):
        all_ref[pl.ds(pl.multiple_of((chip ^ k) * mine, mine), mine), :] = piece[...]
    out_ref[...] = lax.dot_general(
        masked_ref[slot].reshape(-1, depth), all_ref[...], (((1,), (1,)), ((), ())), preferred_element_type=jnp.float32
    ).reshape(out_ref.shape)


def chip_of(index, bits):
    return sum(((index >> (len(bits) - 1 - i)) & 1) << b for i, b in enumerate(bits))


def pack(values, out_ref):
    rows = values[0].shape[0]
    largest = functools.reduce(jnp.maximum, [jnp.max(jnp.abs(v), axis=0, keepdims=True) for v in values])
    exponent = jnp.ceil(jnp.log2(jnp.maximum(largest, 2.0**-110)) + 0.01)
    factor = jnp.exp2(15.0 - exponent)
    for i, value in enumerate(values):
        out_ref[i * rows : (i + 1) * rows] = jnp.round(value * factor).astype(jnp.int32).astype(jnp.int16)
    last = (EXTRA, exponent.shape[1])
    out_ref[len(values) * rows :] = jnp.broadcast_to(exponent, last).astype(jnp.int32).astype(jnp.int16)


def unpack(got_ref):
    stop = got_ref.shape[0] - EXTRA
    exponent = got_ref[stop:].astype(jnp.int32).astype(jnp.float32)[:1]
    step = jnp.exp2(exponent - 15.0)
    return [got_ref[i : i + TILE].astype(jnp.int32).astype(jnp.float32) * step for i in range(0, stop, TILE)]


def packed(blocks, columns):
    return jax.ShapeDtypeStruct((blocks * TILE + EXTRA, columns), jnp.int16)


def plain(blocks, columns):
    return jax.ShapeDtypeStruct((blocks, TILE, columns), jnp.float32)


def first_kernel(bits, keep_ref, got_ref, send, keep):
    half = keep.shape[0]
    sums = []
    for index in range(2 * half):
        k = chip_of(index, bits)
        sums.append(keep_ref[k] + got_ref[k])
    for index in range(half):
        keep[index] = sums[index]
    pack(sums[half:], send)


def halve_kernel(keep_ref, got_ref, send, keep):
    half = keep.shape[0]
    got = unpack(got_ref)
    for index in range(half):
        keep[index] = keep_ref[index] + got[index]
    pack([keep_ref[index] + got[index] for index in range(half, 2 * half)], send)


def place_kernel(chips, me_ref, places_ref, out_ref):
    pairs, columns = places_ref.shape[0] // 2, out_ref.shape[1]
    far = me_ref[0] >= chips
    column = lax.broadcasted_iota(jnp.int32, (pairs, columns), 1)
    low, high = places_ref[:pairs], places_ref[pairs:]
    for c, place in enumerate((jnp.where(far, high, low), jnp.where(far, low, high))):
        ones = (place == column).astype(jnp.float32).astype(out_ref.dtype)
        for part in range(3):
            start = (3 * c + part) * pairs
            out_ref[start : start + pairs] = ones


def last_kernel(near_keep, near_got, far_keep, far_got, place_ref, out_ref):
    parts = []
    for keep_ref, got_ref in ((near_keep, far_got), (far_keep, near_got)):
        rest = keep_ref[0] + unpack(got_ref)[0]
        for _ in range(3):
            parts.append(rest.astype(jnp.bfloat16))
            rest = rest - parts[-1].astype(jnp.float32)
    out_ref[...] = jnp.dot(jnp.concatenate(parts, axis=1), place_ref[...], preferred_element_type=jnp.float32)


def per_device(devices, amplitudes, integrals, block_mask, pair_list):
    me = lax.axis_index("ab").reshape(1)
    chips = devices // 2
    mine, depth = amplitudes.shape[0], integrals.shape[1]
    pairs = mine * chips
    kind = amplitudes.dtype

    def swap(value, bits):
        return lax.ppermute(value, "ab", [(i, i ^ bits) for i in range(devices)])

    block = jax.ShapeDtypeStruct((chips, mine, depth), kind)
    send, keep = call(sort_kernel, "sort", [block] * 2, me, amplitudes, scalars=1)
    got = swap(send, 1)
    piece = jax.ShapeDtypeStruct((2 * mine, depth), kind)
    pieces = call(piece_kernel, "pieces", [piece] * chips, me, keep, got, scalars=1)
    received = {0: pieces[0]}
    for k in sending(chips):
        received[k] = swap(pieces[k], 2 * k)
    begun = lax.optimization_barrier((me, received[chips - 1]))[0]
    masked = masked_rows(begun, block_mask, integrals)

    place = call(
        functools.partial(place_kernel, chips), "place", [jax.ShapeDtypeStruct((6 * pairs, 2 * pairs), kind)],
        begun, pair_list.reshape(-1, 1), scalars=1,
    )[0]

    half = chips // 2
    bits = tuple(range((chips - 1).bit_length()))

    sums = []
    for first, order in ((0, bits), (half, bits[-2::-1] + bits[-1:])):
        send, keep = [
            call(
                functools.partial(product_kernel, slot), "product", [plain(chips, pairs)], me, masked,
                *[received[k] for k in range(first, first + half)], scalars=1,
                scratch=[pltpu.VMEM((pairs, depth), kind)],
            )[0]
            for slot in range(2)
        ]
        me = lax.optimization_barrier((me, keep))[0]
        got = swap(send, 1)
        blocks = half
        send, keep = call(
            functools.partial(first_kernel, order), "core_sum", [packed(blocks, pairs), plain(blocks, pairs)],
            keep, got,
        )
        for bit in order:
            got = swap(send, 2 << bit)
            if blocks > 1:
                blocks //= 2
                send, keep = call(
                    halve_kernel, "halve", [packed(blocks, pairs), plain(blocks, pairs)],
                    keep, got,
                )
        sums += [keep, got]
    return call(last_kernel, "last", [jax.ShapeDtypeStruct((TILE, 2 * pairs), jnp.float32)], *sums, place)[0]


def solution(mesh):
    placed = (P(("groups", "ab"), None), P("groups", "ab"), P("groups", "ab"), P("groups"))
    return jax.shard_map(
        functools.partial(per_device, mesh.shape["ab"]),
        mesh=mesh, in_specs=placed, out_specs=P(("groups", "ab"), None), check_vma=False,
    )
```

```python
import functools

import jax
import jax.numpy as jnp
from jax import lax
from jax.experimental import pallas as pl
from jax.experimental.pallas import tpu as pltpu
from jax.sharding import PartitionSpec as P

TILE = 128
EXTRA = 16


def sending(chips):
    return [chips - 1] + list(range(1, chips // 2)) + list(reversed(range(chips // 2, chips - 1)))


WHOLE = pl.BlockSpec(memory_space=pltpu.VMEM)
SCALARS = pl.BlockSpec(memory_space=pltpu.SMEM)


def call(kernel, name, outs, *args, scalars=0, scratch=(), flops=0):
    moved = sum(a.size * a.dtype.itemsize for a in (*args, *outs))
    return pl.pallas_call(
        kernel,
        out_shape=outs,
        in_specs=[SCALARS] * scalars + [WHOLE] * (len(args) - scalars),
        out_specs=[WHOLE] * len(outs),
        scratch_shapes=list(scratch),
        name=name,
        compiler_params=pltpu.CompilerParams(vmem_limit_bytes=40 * 2**20),
        cost_estimate=pl.CostEstimate(flops=flops, bytes_accessed=moved, transcendentals=0),
    )(*args)


def sort_kernel(me_ref, amplitudes_ref, send_ref, keep_ref):
    chips, _, depth = keep_ref.shape
    chip, core = me_ref[0] // 2, me_ref[0] % 2
    for k in range(chips):
        for out_ref, to in ((send_ref, 1 - core), (keep_ref, core)):
            start = pl.multiple_of(((chip ^ k) * 2 + to) * depth, depth)
            out_ref[k] = amplitudes_ref[:, pl.ds(start, depth)]


def piece_kernel(me_ref, keep_ref, got_ref, *outs):
    mine = keep_ref.shape[1]
    core = me_ref[0] % 2

    def store(first, second):
        for k, out in enumerate(outs):
            out[:mine] = first[k]
            out[mine:] = second[k]

    pl.when(core == 0)(lambda: store(keep_ref, got_ref))
    pl.when(core == 1)(lambda: store(got_ref, keep_ref))


def mask_kernel(me_ref, mask_ref, rows_ref, out_ref, block_ref, arrived):
    chips, _, depth = block_ref.shape
    chip, core = me_ref[0] // 2, me_ref[0] % 2

    def copy(k):
        start = pl.multiple_of((chip ^ k) * (2 * TILE), 2 * TILE)
        return pltpu.make_async_copy(rows_ref.at[pl.ds(start, 2 * TILE), :], block_ref.at[k], arrived.at[k])

    for k in range(chips):
        copy(k).start()

    @pl.loop(0, chips)
    def _(k):
        copy(k).wait()
        for slot, own in enumerate((1 - core, core)):
            rows = pl.ds(pl.multiple_of(own * TILE, TILE), TILE)
            for t in range(mask_ref.shape[1]):
                columns = slice(t * TILE, (t + 1) * TILE)
                factor = mask_ref[(chip ^ k) * 2 + own, t].astype(jnp.float32).astype(out_ref.dtype)
                out_ref[slot, k, :, columns] = block_ref[k, rows, columns] * factor


def masked_rows(me, block_mask, integrals):
    rows, depth = integrals.shape
    chips = rows // (2 * TILE)
    return pl.pallas_call(
        mask_kernel,
        in_specs=[SCALARS, SCALARS, pl.BlockSpec(memory_space=pltpu.HBM)],
        out_specs=WHOLE,
        out_shape=jax.ShapeDtypeStruct((2, chips, TILE, depth), integrals.dtype),
        scratch_shapes=[pltpu.VMEM((chips, 2 * TILE, depth), integrals.dtype), pltpu.SemaphoreType.DMA((chips,))],
        name="mask",
        compiler_params=pltpu.CompilerParams(vmem_limit_bytes=40 * 2**20),
        cost_estimate=pl.CostEstimate(flops=rows * depth, bytes_accessed=4 * rows * depth, transcendentals=0),
    )(me, block_mask, integrals)


def product_kernel(slot, me_ref, masked_ref, *refs):
    *pieces, out_ref, all_ref = refs
    mine, depth = pieces[0].shape
    chip = me_ref[0] // 2 % len(pieces)
    for k, piece in enumerate(pieces):
        all_ref[pl.ds(pl.multiple_of((chip ^ k) * mine, mine), mine), :] = piece[...]
    out_ref[...] = lax.dot_general(
        masked_ref[slot].reshape(-1, depth), all_ref[...], (((1,), (1,)), ((), ())), preferred_element_type=jnp.float32
    ).reshape(out_ref.shape)


def chip_of(index, bits):
    return sum(((index >> (len(bits) - 1 - i)) & 1) << b for i, b in enumerate(bits))


def pack(values, out_ref):
    rows = values[0].shape[0]
    largest = functools.reduce(jnp.maximum, [jnp.max(jnp.abs(v), axis=0, keepdims=True) for v in values])
    exponent = jnp.ceil(jnp.log2(jnp.maximum(largest, 2.0**-110)) + 0.01)
    factor = jnp.exp2(15.0 - exponent)
    for i, value in enumerate(values):
        out_ref[i * rows : (i + 1) * rows] = jnp.round(value * factor).astype(jnp.int32).astype(jnp.int16)
    last = (EXTRA, exponent.shape[1])
    out_ref[len(values) * rows :] = jnp.broadcast_to(exponent, last).astype(jnp.int32).astype(jnp.int16)


def unpack(got_ref):
    stop = got_ref.shape[0] - EXTRA
    exponent = got_ref[stop:].astype(jnp.int32).astype(jnp.float32)[:1]
    step = jnp.exp2(exponent - 15.0)
    return [got_ref[i : i + TILE].astype(jnp.int32).astype(jnp.float32) * step for i in range(0, stop, TILE)]


def packed(blocks, columns):
    return jax.ShapeDtypeStruct((blocks * TILE + EXTRA, columns), jnp.int16)


def plain(blocks, columns):
    return jax.ShapeDtypeStruct((blocks, TILE, columns), jnp.float32)


def first_kernel(bits, keep_ref, got_ref, send, keep):
    half = keep.shape[0]
    sums = []
    for index in range(2 * half):
        k = chip_of(index, bits)
        sums.append(keep_ref[k] + got_ref[k])
    for index in range(half):
        keep[index] = sums[index]
    pack(sums[half:], send)


def halve_kernel(keep_ref, got_ref, send, keep):
    half = keep.shape[0]
    got = unpack(got_ref)
    for index in range(half):
        keep[index] = keep_ref[index] + got[index]
    pack([keep_ref[index] + got[index] for index in range(half, 2 * half)], send)


def place_kernel(chips, me_ref, places_ref, out_ref):
    pairs, columns = places_ref.shape[0] // 2, out_ref.shape[1]
    far = me_ref[0] >= chips
    column = lax.broadcasted_iota(jnp.int32, (pairs, columns), 1)
    low, high = places_ref[:pairs], places_ref[pairs:]
    for c, place in enumerate((jnp.where(far, high, low), jnp.where(far, low, high))):
        ones = (place == column).astype(jnp.float32).astype(out_ref.dtype)
        for part in range(3):
            start = (3 * c + part) * pairs
            out_ref[start : start + pairs] = ones


def split_kernel(keep_ref, got_ref, *outs):
    got = unpack(got_ref)
    for index, out in enumerate(outs):
        if index:
            pack([keep_ref[index] + got[index]], out)
        else:
            out[0] = keep_ref[0] + got[0]


def last_kernel(counts, *refs):
    *sums, place_ref, out_ref = refs
    parts, start = [], 2
    received = []
    for count in counts:
        received.append(sums[start : start + count])
        start += count
    for c in range(2):
        rest = sums[c][0]
        for got_ref in received[c]:
            rest += unpack(got_ref)[0]
        for _ in range(3):
            parts.append(rest.astype(jnp.bfloat16))
            rest = rest - parts[-1].astype(jnp.float32)
    out_ref[...] = jnp.dot(jnp.concatenate(parts, axis=1), place_ref[...], preferred_element_type=jnp.float32)


def per_device(devices, amplitudes, integrals, block_mask, pair_list):
    me = lax.axis_index("ab").reshape(1)
    chips = devices // 2
    mine, depth = amplitudes.shape[0], integrals.shape[1]
    pairs = mine * chips
    kind = amplitudes.dtype

    def swap(value, bits):
        return lax.ppermute(value, "ab", [(i, i ^ bits) for i in range(devices)])

    block = jax.ShapeDtypeStruct((chips, mine, depth), kind)
    send, keep = call(sort_kernel, "sort", [block] * 2, me, amplitudes, scalars=1)
    got = swap(send, 1)
    piece = jax.ShapeDtypeStruct((2 * mine, depth), kind)
    pieces = call(piece_kernel, "pieces", [piece] * chips, me, keep, got, scalars=1)
    received = {0: pieces[0]}
    for k in sending(chips):
        received[k] = swap(pieces[k], 2 * k)
    begun = lax.optimization_barrier((me, received[chips - 1]))[0]
    masked = masked_rows(begun, block_mask, integrals)

    place = call(
        functools.partial(place_kernel, chips), "place", [jax.ShapeDtypeStruct((6 * pairs, 2 * pairs), kind)],
        begun, pair_list.reshape(-1, 1), scalars=1,
    )[0]

    half = chips // 2
    bits = tuple(range((chips - 1).bit_length()))

    sums, parts = [], ([], [])
    for first, order in ((0, bits[-2::-1] + bits[-1:]), (half, bits)):
        send, keep = [
            call(
                functools.partial(product_kernel, slot), "product", [plain(chips, pairs)], me, masked,
                *[received[k] for k in range(first, first + half)], scalars=1,
                scratch=[pltpu.VMEM((pairs, depth), kind)],
            )[0]
            for slot in range(2)
        ]
        me = lax.optimization_barrier((me, keep))[0]
        got = swap(send, 1)
        blocks = half
        send, keep = call(
            functools.partial(first_kernel, order), "core_sum", [packed(blocks, pairs), plain(blocks, pairs)],
            keep, got,
        )
        which = 0 if first == 0 else 1
        for bit in order[:-2]:
            got = swap(send, 2 << bit)
            if blocks > 4:
                blocks //= 2
                send, keep = call(halve_kernel, "halve", [packed(blocks, pairs), plain(blocks, pairs)], keep, got)
        one, last = 2 << order[-2], 2 << order[-1]
        if which in (1,):
            keep, *sends = call(
                split_kernel, "split", [plain(1, pairs)] + [packed(1, pairs)] * 3, keep, got
            )
            for send, to in zip(sends, (last, one, one + last), strict=True):
                parts[which ^ (to >= last)].append(swap(send, to))
        else:
            send, keep = call(halve_kernel, "halve", [packed(2, pairs), plain(2, pairs)], keep, got)
            got = swap(send, one)
            send, keep = call(halve_kernel, "halve", [packed(1, pairs), plain(1, pairs)], keep, got)
            parts[1 - which].append(swap(send, last))
        sums.append(keep)
    return call(
        functools.partial(last_kernel, [len(p) for p in parts]), "last",
        [jax.ShapeDtypeStruct((TILE, 2 * pairs), jnp.float32)], *sums, *parts[0], *parts[1], place,
    )[0]


def solution(mesh):
    placed = (P(("groups", "ab"), None), P("groups", "ab"), P("groups", "ab"), P("groups"))
    return jax.shard_map(
        functools.partial(per_device, mesh.shape["ab"]),
        mesh=mesh, in_specs=placed, out_specs=P(("groups", "ab"), None), check_vma=False,
    )
```
